768 devices in a mesh: grp: 12 (over z), sub: 64 (over y, x, core).
Axes of the slice: x: 4, y: 8, z: 12, core: 2. Of those that a mesh axis runs over, the one named last changes fastest.
Arguments:
- basis_values: bfloat16 [12288, 256, 512], P(('grp', 'sub')), may hold values from -6 to 6
- core_density: float32 [12288, 256], P(('grp', 'sub')), may hold values from 0.3 to 3
- weights: float32 [12288, 256], P(('grp', 'sub')), may hold values from 0.00025 to 0.0045
- density_blocks: bfloat16 [1536, 128, 128], P(('grp', 'sub')), may hold values from -0.01171875 to 0.01171875
- pair_block: int32 [3072, 16], P(('grp', 'sub')), may hold values from 0 to 127, as said below
- batch_set: int32 [12288], P(('grp', 'sub')), may hold values from 0 to 3
Outputs:
- hamiltonian: float32 [1536, 128, 128], P(('grp', 'sub'))
The draws below stay inside these ranges and needn't reach their ends.
Inputs may be any that keep to these rules, and one draw needn't show every extreme that they name: `pair_block`: entry v names stored block v % 2 of the device with index v // 2 along sub in the set's group. The 64 entries of one device's sets name blocks of each device of its group exactly 1 times.
All inputs are finite; a program needn't handle non-finite values.
Results may differ from the reference program's by a relative error of at most 0.0018.
Values may be sent and summed in bfloat16 or wider, within the bound.
No kernel may reach another device: no remote copies, remote signals or barrier semaphores. Data moves between devices by JAX's collectives and lax.ppermute only.
A program may use at most 32 MiB of HBM per device.

```python
import math
import jax
import jax.numpy as jnp
from jax import lax

TILE = 128
SET_TILES = 4
P_SIZE = 256
B_DEV = 16
SETS_DEV = 4
TILE_DEV = 2
PAIRS = 16
WIDTH = 512
BATCHES = 12288
SETS = 3072
GROUP_BLOCKS = 128
BLOCKS = 1536
ELECTRONS = 6144
N_GRP = 12
N_SUB = 64


def draw_weights(key, part):
    key = jax.random.fold_in(key, 11)
    growth = 1.0 + 2.0 * jnp.arange(BATCHES, dtype=jnp.float32)[:, None] / BATCHES
    base_values = jax.random.uniform(key, (BATCHES, P_SIZE), jnp.float32, 0.5, 1.5)
    return (0.001 * base_values * growth).astype(jnp.float32)


def draw_pair_block(key, part):
    key = jax.random.fold_in(key, 7)
    devices = N_GRP * N_SUB
    request_count = SETS_DEV * PAIRS
    device_keys = jax.random.split(key, devices)
    shuffled = jax.vmap(lambda device_key: jax.random.permutation(device_key, request_count))(device_keys)
    owner_index = shuffled.astype(jnp.int32) % N_SUB
    local_slot = jax.random.randint(jax.random.fold_in(key, 1), (devices, request_count), 0, TILE_DEV, dtype=jnp.int32)
    return (owner_index * TILE_DEV + local_slot).astype(jnp.int32).reshape(SETS, PAIRS)


def plant(array, key, least, high):
    longest = array.shape.index(max(array.shape))
    spots = []
    for shift in (0, 1):
        where = [jax.random.randint(jax.random.fold_in(key, axis), (), 0, length) for axis, length in enumerate(array.shape)]
        where[longest] = (where[longest] + shift) % array.shape[longest]
        spots.append(tuple(where))
    return array.at[spots[0]].set(least).at[spots[1]].set(high)


def block_scale(stream_key, dims, shards, least, largest):
    gain = 1.0
    for axis_at, shards_of in shards:
        heights = jax.random.uniform(jax.random.fold_in(jax.random.fold_in(stream_key, 6), axis_at), (shards_of,), jnp.float32, least / len(shards), largest / len(shards))
        gain = gain * jnp.repeat(jnp.exp(heights), dims[axis_at] // shards_of).reshape((-1,) + (1,) * (len(dims) - 1 - axis_at))
    return gain


def normal_values(rng, dims, scale, most, cuts=(), held_as=jnp.bfloat16):
    drawn = scale * jax.random.normal(rng, dims, jnp.float32)
    if cuts:
        drawn = drawn * block_scale(rng, dims, cuts, -0.22, 0.18)
    return jnp.clip(drawn, -most, most).astype(held_as)


def setup_inputs(seed: int = 0) -> dict:
    key_of = jax.random.split(jax.random.key(seed), 7)
    basis_values = normal_values(key_of[0], (BATCHES, P_SIZE, WIDTH), 1.0, 6.0, ((0, 768),))
    core_density = jnp.clip(jnp.exp(math.log(3.0) - 2.3025851 * jax.random.uniform(key_of[1], (BATCHES, P_SIZE), jnp.float32) ** block_scale(key_of[1], (BATCHES, P_SIZE), ((0, 768),), -0.2, 0.2)), 0.3, 3.0)
    weights = draw_weights(jax.random.fold_in(key_of[6], 71), 0)
    density_blocks = normal_values(key_of[3], (BLOCKS, TILE, TILE), (1.0 / WIDTH), 0.01171875, ((0, 768),))
    pair_block = draw_pair_block(jax.random.fold_in(key_of[6], 71), 0)
    batch_set = plant(jax.random.randint(key_of[5], (BATCHES,), 0, SETS_DEV), jax.random.fold_in(key_of[5], 1), 0, SETS_DEV - 1).astype(jnp.int32)
    return dict(basis_values=basis_values, core_density=core_density, weights=weights, density_blocks=density_blocks, pair_block=pair_block, batch_set=batch_set)


slater_factor = (3.0 / math.pi) ** (1.0 / 3.0)
density_floor = 0.1


def assemble(tile_stack, tile_count, tile_edge):
    tile_grid = tile_stack.reshape(tile_count, tile_count, tile_edge, tile_edge)
    return tile_grid.transpose(0, 2, 1, 3).reshape(tile_count * tile_edge, tile_count * tile_edge)


def split_tiles(whole_matrix, tile_count, tile_edge):
    tile_grid = whole_matrix.reshape(tile_count, tile_edge, tile_count, tile_edge)
    return tile_grid.transpose(0, 2, 1, 3).reshape(tile_count * tile_count, tile_edge, tile_edge)


def reference(basis_values, core_density, weights, density_blocks, pair_block, batch_set):
    devices = N_GRP * N_SUB
    basis_width = SET_TILES * TILE
    values_dev = basis_values.reshape(devices, B_DEV, P_SIZE, basis_width)
    set_dev = batch_set.reshape(devices, B_DEV).astype(jnp.int32)
    group_base = (jnp.arange(devices, dtype=jnp.int32) // N_SUB) * GROUP_BLOCKS
    block_dev = pair_block.reshape(devices, SETS_DEV, PAIRS).astype(jnp.int32) + group_base[:, None, None]

    def device_density(packed):
        values, set_ids, block_ids = packed
        set_matrices = jnp.stack([assemble(density_blocks[block_ids[member]], SET_TILES, TILE) for member in range(SETS_DEV)])
        chosen = set_matrices[set_ids].astype(jnp.float32)
        values_float = values.astype(jnp.float32)
        mixed_rows = jnp.einsum("bpi,bij->bpj", values_float, chosen)
        return jnp.sum(mixed_rows * values_float, axis=2)

    valence = lax.map(device_density, (values_dev, set_dev, block_dev))
    density = jnp.maximum(core_density.reshape(devices, B_DEV, P_SIZE) + valence, density_floor)
    weight_rows = weights.reshape(devices, B_DEV, P_SIZE)
    charge = jnp.sum(weight_rows * density)
    scale_factor = jnp.cbrt(ELECTRONS / charge)
    potential = -slater_factor * jnp.cbrt(density) * weight_rows * scale_factor

    def accumulate(running, packed):
        values, potential_rows, set_ids, block_ids = packed
        values_float = values.astype(jnp.float32)
        weighted = (potential_rows[:, :, None] * values_float).astype(jnp.bfloat16)
        weighted = lax.optimization_barrier(weighted).astype(jnp.float32)
        per_batch = jnp.einsum("bpi,bpj->bij", values_float, weighted)
        onehot = (set_ids[:, None] == jnp.arange(SETS_DEV, dtype=jnp.int32)[None, :]).astype(jnp.float32)
        per_set = jnp.einsum("bq,bij->qij", onehot, per_batch, precision=lax.Precision.HIGHEST)
        partial_value = jnp.concatenate([split_tiles(per_set[member], SET_TILES, TILE) for member in range(SETS_DEV)]).astype(jnp.bfloat16)
        partial_value = lax.optimization_barrier(partial_value).astype(jnp.float32)
        return running.at[block_ids.reshape(-1)].add(partial_value), None

    hamiltonian, unused = lax.scan(accumulate, jnp.zeros((BLOCKS, TILE, TILE), jnp.float32), (values_dev, potential, set_dev, block_dev))
    return hamiltonian
```

```python
import math

import jax
import jax.numpy as jnp
from jax import lax
from jax.experimental import pallas as pl
from jax.experimental.pallas import tpu as pltpu
from jax.sharding import Mesh, PartitionSpec as P

slater_factor = (3.0 / math.pi) ** (1.0 / 3.0)
density_floor = 0.1

Y, X, C = 8, 4, 2
SUB = Y * X * C
TILE = 128
TILES = 4
WIDTH = TILES * TILE
PAIRS = TILES * TILES
SETS = 4
REQUESTS = SETS * PAIRS
BATCHES = 16
POINTS = 256
LOCAL = 2
EXTRA = 16
ROWS = LOCAL * TILE + EXTRA


def cube_root(value):
    return jnp.exp2(jnp.log2(value) * (1.0 / 3.0))


def transpose_kernel(values_ref, flipped_ref):
    flipped_ref[0] = values_ref[0].T


def batch_kernel(
    pair_ref,
    set_ref,
    core_ref,
    near_ref,
    far_ref,
    values_ref,
    flipped_ref,
    core_density_ref,
    weights_ref,
    tiles_ref,
    charge_ref,
    matrices,
    valence,
    potential,
    totals,
):
    my_core = core_ref[0]
    for k in range(REQUESTS):
        wanted = pair_ref[k]
        owner = wanted // LOCAL
        slot = wanted % LOCAL
        y, x, c = owner // (X * C), (owner // C) % X, owner % C
        s, a, b = k // PAIRS, (k // TILES) % TILES, k % TILES
        rows = pl.ds(pl.multiple_of(slot * TILE, TILE), TILE)
        near = near_ref[x, y, rows, :]
        far = far_ref[x, y, rows, :]
        matrices[s, a * TILE : (a + 1) * TILE, b * TILE : (b + 1) * TILE] = jnp.where(
            c == my_core, near, far
        )

    def batch_valence(b, carry):
        flipped = flipped_ref[b]
        mixed = jnp.dot(matrices[set_ref[b]], flipped, preferred_element_type=jnp.float32)
        valence[pl.ds(b, 1), :] = jnp.sum(
            mixed * flipped.astype(jnp.float32), axis=0, keepdims=True
        )
        return carry

    lax.fori_loop(0, BATCHES, batch_valence, 0, unroll=2)
    density = jnp.maximum(core_density_ref[...] + valence[...], density_floor)
    weights = weights_ref[...]
    charge_ref[...] = jnp.broadcast_to(jnp.sum(weights * density), charge_ref.shape)
    potential[...] = -slater_factor * cube_root(density) * weights
    totals[...] = jnp.zeros_like(totals)

    def batch_integral(b, carry):
        weighted = (flipped_ref[b].astype(jnp.float32) * potential[pl.ds(b, 1), :]).astype(
            jnp.bfloat16
        )
        totals[set_ref[b]] += jnp.dot(
            weighted, values_ref[b], preferred_element_type=jnp.float32
        )
        return carry

    lax.fori_loop(0, BATCHES, batch_integral, 0, unroll=2)
    for k in range(REQUESTS):
        owner = pair_ref[k] // LOCAL
        s, a, b = k // PAIRS, (k // TILES) % TILES, k % TILES
        tiles_ref[owner] = totals[
            s, a * TILE : (a + 1) * TILE, b * TILE : (b + 1) * TILE
        ].astype(jnp.bfloat16)


def sum_kernel(electrons, slot_ref, tiles_ref, charge_ref, out_ref):
    charge = jnp.sum(charge_ref[:, 0:1, :], axis=0)
    scale = cube_root(electrons / charge)
    out_ref[...] = jnp.zeros_like(out_ref)
    for d in range(SUB):
        out_ref[slot_ref[d]] += tiles_ref[d].astype(jnp.float32)
    out_ref[...] = out_ref[...] * scale[None]


def body(basis_values, core_density, weights, density_blocks, pair_block, batch_set):
    vmem = pl.BlockSpec(memory_space=pltpu.VMEM)
    smem = pl.BlockSpec(memory_space=pltpu.SMEM)
    params = pltpu.CompilerParams(vmem_limit_bytes=56 * 1024 * 1024)
    y, x, c = lax.axis_index("y"), lax.axis_index("x"), lax.axis_index("c")
    me = (y * X + x) * C + c
    wanted = pair_block.reshape(REQUESTS)
    lanes = jnp.arange(TILE, dtype=jnp.int32)
    slots = jnp.sum(
        jnp.where((wanted // LOCAL)[:, None] == lanes[None, :], (wanted % LOCAL)[:, None], 0), axis=0
    ).astype(jnp.bfloat16)
    payload = jnp.concatenate(
        [density_blocks.reshape(LOCAL * TILE, TILE), jnp.broadcast_to(slots[None, :], (EXTRA, TILE))]
    )
    column = lax.all_to_all(
        jnp.broadcast_to(payload[None], (Y, ROWS, TILE)), "y", split_axis=0, concat_axis=0, tiled=True
    )
    near = lax.all_to_all(
        jnp.broadcast_to(column[None], (X, Y, ROWS, TILE)),
        "x",
        split_axis=0,
        concat_axis=0,
        tiled=True,
    )
    far = lax.ppermute(near, "c", [(0, 1), (1, 0)])

    flipped = pl.pallas_call(
        transpose_kernel,
        grid=(BATCHES,),
        in_specs=[pl.BlockSpec((1, POINTS, WIDTH), lambda b: (b, 0, 0))],
        out_specs=pl.BlockSpec((1, WIDTH, POINTS), lambda b: (b, 0, 0)),
        out_shape=jax.ShapeDtypeStruct((BATCHES, WIDTH, POINTS), jnp.bfloat16),
    )(basis_values)

    tiles, charge = pl.pallas_call(
        batch_kernel,
        in_specs=[smem, smem, smem, vmem, vmem, vmem, vmem, vmem, vmem],
        out_specs=[vmem, vmem],
        out_shape=[
            jax.ShapeDtypeStruct((SUB, TILE, TILE), jnp.bfloat16),
            jax.ShapeDtypeStruct((12, 8, TILE), jnp.float32),
        ],
        scratch_shapes=[
            pltpu.VMEM((SETS, WIDTH, WIDTH), jnp.bfloat16),
            pltpu.VMEM((BATCHES, POINTS), jnp.float32),
            pltpu.VMEM((BATCHES, POINTS), jnp.float32),
            pltpu.VMEM((SETS, WIDTH, WIDTH), jnp.float32),
        ],
        compiler_params=params,
    )(wanted, batch_set, c.reshape(1), near, far, basis_values, flipped, core_density, weights)

    returned = lax.all_to_all(tiles, ("y", "x", "c"), split_axis=0, concat_axis=0, tiled=True)
    column_charge = lax.all_to_all(charge, "grp", split_axis=0, concat_axis=0, tiled=True)
    column_charge = jnp.broadcast_to(jnp.sum(column_charge, axis=0)[None], (SUB, 8, TILE))
    group_charge = lax.all_to_all(
        column_charge, ("y", "x", "c"), split_axis=0, concat_axis=0, tiled=True
    )
    near_slots = near[:, :, LOCAL * TILE, :]
    far_slots = far[:, :, LOCAL * TILE, :]
    both = jnp.where(
        (c == jnp.arange(C, dtype=jnp.int32))[:, None, None, None], near_slots[None], far_slots[None]
    )
    mine = jnp.sum(jnp.where(lanes == me, both, 0), axis=-1, dtype=jnp.float32)
    slot_of = mine.transpose(2, 1, 0).reshape(SUB).astype(jnp.int32)
    electrons = float(POINTS * BATCHES * 12 * SUB // 512)

    def summed(slot_ref, tiles_ref, charge_ref, out_ref):
        sum_kernel(electrons, slot_ref, tiles_ref, charge_ref, out_ref)

    return pl.pallas_call(
        summed,
        in_specs=[smem, vmem, vmem],
        out_specs=vmem,
        out_shape=jax.ShapeDtypeStruct((LOCAL, TILE, TILE), jnp.float32),
        compiler_params=params,
    )(slot_of, returned, group_charge)


def solution(mesh):
    split = Mesh(mesh.devices.reshape(12, Y, X, C), ("grp", "y", "x", "c"))
    every = ("grp", "y", "x", "c")
    placed = (
        P(every, None, None),
        P(every, None),
        P(every, None),
        P(every, None, None),
        P(every, None),
        P(every),
    )
    return jax.shard_map(
        body, mesh=split, in_specs=placed, out_specs=P(every, None, None), check_vma=False
    )
```

```python
import math

import jax
import jax.numpy as jnp
from jax import lax
from jax.experimental import pallas as pl
from jax.experimental.pallas import tpu as pltpu
from jax.sharding import Mesh, PartitionSpec as P

slater_factor = (3.0 / math.pi) ** (1.0 / 3.0)
density_floor = 0.1

Y, X, C = 8, 4, 2
SUB = Y * X * C
TILE = 128
TILES = 4
WIDTH = TILES * TILE
PAIRS = TILES * TILES
SETS = 4
REQUESTS = SETS * PAIRS
BATCHES = 16
POINTS = 256
LOCAL = 2
ROWS = LOCAL * TILE
CHARGE_LANE = TILE - 1
GROUP = 8


def cube_root(value):
    return jnp.exp2(jnp.log2(value) * (1.0 / 3.0))


def transpose_kernel(values_ref, flipped_ref):
    for b in range(values_ref.shape[0]):
        flipped_ref[b] = values_ref[b].T


def batch_kernel(
    pair_ref,
    set_ref,
    core_ref,
    near_ref,
    far_ref,
    values_ref,
    flipped_ref,
    core_density_ref,
    weights_ref,
    tiles_ref,
    charge_ref,
    matrices,
    values,
    flipped,
    valence,
    potential,
    totals,
    rounded,
    tile_sem,
    value_sems,
    flip_sems,
    out_sem,
):
    my_core = core_ref[0]

    def fetch(source, target, sems, g):
        part = pl.ds(g * GROUP, GROUP)
        return pltpu.make_async_copy(source.at[part], target.at[part], sems.at[g])

    fetch(flipped_ref, flipped, flip_sems, 0).start()

    def fetch_tile(k, carry):
        wanted = pair_ref[k]
        owner = wanted // LOCAL
        y, x, c = owner // (X * C), (owner // C) % X, owner % C
        rows = pl.ds(pl.multiple_of((wanted % LOCAL) * TILE, TILE), TILE)
        into = matrices.at[
            k // PAIRS,
            pl.ds(pl.multiple_of((k // TILES) % TILES * TILE, TILE), TILE),
            pl.ds(pl.multiple_of(k % TILES * TILE, TILE), TILE),
        ]

        @pl.when(c == my_core)
        def _():
            pltpu.make_async_copy(near_ref.at[x, y, rows, :], into, tile_sem).start()

        @pl.when(c != my_core)
        def _():
            pltpu.make_async_copy(far_ref.at[x, y, rows, :], into, tile_sem).start()

        return carry

    lax.fori_loop(0, REQUESTS, fetch_tile, 0, unroll=8)
    for g in range(1, BATCHES // GROUP):
        fetch(flipped_ref, flipped, flip_sems, g).start()
    for g in range(BATCHES // GROUP):
        fetch(values_ref, values, value_sems, g).start()
    totals[...] = jnp.zeros_like(totals)
    pltpu.make_async_copy(matrices, matrices, tile_sem).wait()

    def group_valence(g, carry):
        fetch(flipped_ref, flipped, flip_sems, g).wait()
        for i in range(GROUP):
            b = g * GROUP + i
            turned = flipped[b]
            mixed = jnp.dot(matrices[set_ref[b]], turned, preferred_element_type=jnp.float32)
            valence[pl.ds(b, 1), :] = jnp.sum(
                mixed * turned.astype(jnp.float32), axis=0, keepdims=True
            )
        return carry

    lax.fori_loop(0, BATCHES // GROUP, group_valence, 0)
    density = jnp.maximum(core_density_ref[...] + valence[...], density_floor)
    weights = weights_ref[...]
    charge_ref[...] = jnp.broadcast_to(jnp.sum(weights * density), charge_ref.shape)
    potential[...] = -slater_factor * cube_root(density) * weights

    def group_integral(g, carry):
        fetch(values_ref, values, value_sems, g).wait()
        for i in range(GROUP):
            b = g * GROUP + i
            weighted = (flipped[b].astype(jnp.float32) * potential[pl.ds(b, 1), :]).astype(
                jnp.bfloat16
            )
            totals[set_ref[b]] += jnp.dot(
                weighted, values[b], preferred_element_type=jnp.float32
            )
        return carry

    lax.fori_loop(0, BATCHES // GROUP, group_integral, 0)
    for k in range(REQUESTS):
        s, a, b = k // PAIRS, (k // TILES) % TILES, k % TILES
        rounded[k] = totals[
            s, a * TILE : (a + 1) * TILE, b * TILE : (b + 1) * TILE
        ].astype(jnp.bfloat16)
        pltpu.make_async_copy(rounded.at[k], tiles_ref.at[pair_ref[k] // LOCAL], out_sem).start()
    pltpu.make_async_copy(rounded, tiles_ref, out_sem).wait()


def sum_kernel(electrons, me_ref, tiles_ref, rows_ref, out_ref, second):
    rows = rows_ref[...]
    charge = jnp.sum(rows[:, CHARGE_LANE:])
    scale = cube_root(jnp.full((1, TILE), electrons, jnp.float32) / charge)
    lane = lax.broadcasted_iota(jnp.int32, (TILE, TILE), 0)
    pick = (lane == me_ref[0]).astype(jnp.bfloat16)
    second[...] = jnp.dot(rows.astype(jnp.bfloat16), pick, preferred_element_type=jnp.float32)
    step = 16
    for r in range(0, TILE, step):
        sums = [jnp.zeros((step, TILE), jnp.float32), jnp.zeros((step, TILE), jnp.float32)]
        for d in range(SUB):
            tile = tiles_ref[d, r : r + step, :].astype(jnp.float32)
            in_second = jnp.broadcast_to(second[d : d + 1, :], tile.shape) > 0.5
            sums[0] += jnp.where(in_second, 0.0, tile)
            sums[1] += jnp.where(in_second, tile, 0.0)
        for slot in range(LOCAL):
            out_ref[slot, r : r + step, :] = sums[slot] * scale


def body(basis_values, core_density, weights, density_blocks, pair_block, batch_set):
    vmem = pl.BlockSpec(memory_space=pltpu.VMEM)
    smem = pl.BlockSpec(memory_space=pltpu.SMEM)
    anywhere = pl.BlockSpec(memory_space=pl.ANY)
    params = pltpu.CompilerParams(vmem_limit_bytes=56 * 1024 * 1024)

    def kept(array):
        return pltpu.with_memory_space_constraint(array, pltpu.VMEM)

    y, x, c = lax.axis_index("y"), lax.axis_index("x"), lax.axis_index("c")
    me = (y * X + x) * C + c
    wanted = pair_block.reshape(REQUESTS)
    column = lax.all_to_all(
        jnp.broadcast_to(density_blocks.reshape(1, ROWS, TILE), (Y, ROWS, TILE)),
        "y",
        split_axis=0,
        concat_axis=0,
        tiled=True,
    )
    near = lax.all_to_all(
        jnp.broadcast_to(column[None], (X, Y, ROWS, TILE)),
        "x",
        split_axis=0,
        concat_axis=0,
        tiled=True,
    )
    flipped = pl.pallas_call(
        transpose_kernel,
        grid=(BATCHES // 2,),
        in_specs=[pl.BlockSpec((2, POINTS, WIDTH), lambda b: (b, 0, 0))],
        out_specs=pl.BlockSpec((2, WIDTH, POINTS), lambda b: (b, 0, 0)),
        out_shape=jax.ShapeDtypeStruct((BATCHES, WIDTH, POINTS), jnp.bfloat16),
        compiler_params=params,
    )(basis_values)
    near, flipped = lax.optimization_barrier((near, flipped))
    far = lax.ppermute(near, "c", [(0, 1), (1, 0)])

    tiles, charge = pl.pallas_call(
        batch_kernel,
        in_specs=[smem, smem, smem, anywhere, anywhere, anywhere, anywhere, vmem, vmem],
        out_specs=[anywhere, vmem],
        out_shape=[
            jax.ShapeDtypeStruct((SUB, TILE, TILE), jnp.bfloat16),
            jax.ShapeDtypeStruct((1, TILE), jnp.float32),
        ],
        scratch_shapes=[
            pltpu.VMEM((SETS, WIDTH, WIDTH), jnp.bfloat16),
            pltpu.VMEM((BATCHES, POINTS, WIDTH), jnp.bfloat16),
            pltpu.VMEM((BATCHES, WIDTH, POINTS), jnp.bfloat16),
            pltpu.VMEM((BATCHES, POINTS), jnp.float32),
            pltpu.VMEM((BATCHES, POINTS), jnp.float32),
            pltpu.VMEM((SETS, WIDTH, WIDTH), jnp.float32),
            pltpu.VMEM((REQUESTS, TILE, TILE), jnp.bfloat16),
            pltpu.SemaphoreType.DMA,
            pltpu.SemaphoreType.DMA((BATCHES // GROUP,)),
            pltpu.SemaphoreType.DMA((BATCHES // GROUP,)),
            pltpu.SemaphoreType.DMA,
        ],
        compiler_params=params,
    )(
        wanted,
        batch_set,
        c.reshape(1),
        near,
        far,
        basis_values,
        flipped,
        core_density,
        weights,
    )

    returned = lax.all_to_all(tiles, ("y", "x", "c"), split_axis=0, concat_axis=0, tiled=True)
    lanes = jnp.arange(TILE, dtype=jnp.int32)
    slots = jnp.sum(
        jnp.where((wanted // LOCAL)[:, None] == lanes[None, :], (wanted % LOCAL)[:, None], 0), axis=0
    ).astype(jnp.float32)
    charge = lax.psum(charge, "grp")
    row = jnp.where(lanes[None, :] == CHARGE_LANE, charge, slots[None, :])
    rows = lax.all_gather(row, ("y", "x", "c"), axis=0, tiled=True)
    electrons = float(POINTS * BATCHES * 12 * SUB // 512)

    def summed(me_ref, tiles_ref, rows_ref, out_ref, second):
        sum_kernel(electrons, me_ref, tiles_ref, rows_ref, out_ref, second)

    return pl.pallas_call(
        summed,
        in_specs=[smem, vmem, vmem],
        out_specs=vmem,
        out_shape=jax.ShapeDtypeStruct((LOCAL, TILE, TILE), jnp.float32),
        scratch_shapes=[pltpu.VMEM((SUB, TILE), jnp.float32)],
        compiler_params=params,
    )(me.reshape(1), kept(returned), rows)


def solution(mesh):
    split = Mesh(mesh.devices.reshape(12, Y, X, C), ("grp", "y", "x", "c"))
    every = ("grp", "y", "x", "c")
    placed = (
        P(every, None, None),
        P(every, None),
        P(every, None),
        P(every, None, None),
        P(every, None),
        P(every),
    )
    return jax.shard_map(
        body, mesh=split, in_specs=placed, out_specs=P(every, None, None), check_vma=False
    )
```
